32 devices in a mesh: group: 2 (over y), dp: 8 (over z, x), shard: 2 (over core).
Axes of the slice: x: 2, y: 2, z: 4, core: 2. Of those that a mesh axis runs over, the one named last changes fastest.
Arguments:
- inputs: bfloat16 [32, 16, 32, 256], P(('group', 'dp', 'shard')), parts along dimension 0, may hold values from -6 to 6
- cotangent: bfloat16 [32, 16, 32, 256], P(('group', 'dp', 'shard')), parts along dimension 0, may hold values from -6 to 6
- conv_first: bfloat16 [18, 256, 256], P('group', None, 'shard'), parts along dimension 0, may hold values from -0.125 to 0.125
- conv_second: bfloat16 [18, 256, 256], P('group', None, 'shard'), parts along dimension 0, may hold values from -0.125 to 0.125
Outputs:
- outputs: bfloat16 [32, 16, 32, 256], P(('group', 'dp', 'shard')), parts along dimension 0
- grad_first: bfloat16 [18, 256, 256], P('group', None, 'shard'), parts along dimension 0
- grad_second: bfloat16 [18, 256, 256], P('group', None, 'shard'), parts along dimension 0
The draws below stay inside these ranges and needn't reach their ends.
There are 2 independent parts, one for each index of `group`. The reference program is written for one: setup_inputs(seed, part) draws one part's arguments, and reference() takes and returns one part's arrays. A program takes and returns all parts, laid end to end along the dimension named above; each array names one. Nothing has to cross between parts.
All inputs are finite; a program needn't handle non-finite values.
Results may differ from the reference program's by a relative error of at most 0.012.
Values may be sent and summed in bfloat16 or wider, within the bound.
No kernel may reach another device: no remote copies, remote signals or barrier semaphores. Data moves between devices by JAX's collectives and lax.ppermute only.
A program may use at most 64 MiB of HBM per device.

```python
import jax
import jax.numpy as jnp
from jax import lax

C = 256
HH = 16
WW = 32
SAMP_DEV = 1
SAMPLES = 16


def block_levels(stream_key, extent, split, low, largest):
    loudness, own = 1.0, jax.random.fold_in(stream_key, 6)
    for axis_at, shards_of in split:
        draws = jnp.exp(jax.random.uniform(jax.random.fold_in(own, axis_at), (shards_of,), jnp.float32, low / len(split), largest / len(split)))
        loudness = loudness * jnp.repeat(draws, extent[axis_at] // shards_of).reshape([-1 if axis == axis_at else 1 for axis in range(len(extent))])
    return loudness


def normal_values(rng, shape, spread, reach, shards=(), held_as=jnp.bfloat16):
    loudness = block_levels(rng, shape, shards, -0.22, 0.18) if shards else 1.0
    values = jax.random.normal(rng, shape, jnp.float32) * spread * loudness
    return jnp.minimum(jnp.maximum(values, -reach), reach).astype(held_as)


def setup_inputs(seed: int = 0, part: int = 0) -> dict:
    splits = jax.random.split(jax.random.key(seed), 5)
    part_splits = jax.random.split(jax.random.fold_in(splits[4], part), 5)
    inputs = normal_values(part_splits[0], (SAMPLES, HH, WW, C), 1.0, 6.0, ((0, 16),))
    cotangent = normal_values(part_splits[1], (SAMPLES, HH, WW, C), 1.0, 6.0, ((0, 16),))
    conv_first = normal_values(part_splits[2], (9, C, C), (9 * C) ** -0.5, 0.125, ((2, 2),))
    conv_second = normal_values(part_splits[3], (9, C, C), (9 * C) ** -0.5, 0.125, ((2, 2),))
    return dict(inputs=inputs, cotangent=cotangent, conv_first=conv_first, conv_second=conv_second)


def conv_taps(field, kernel):
    samples, rows, cols, chans = field.shape
    padded = jnp.pad(field, ((0, 0), (1, 1), (1, 1), (0, 0)))
    total = jnp.zeros((samples * rows * cols, kernel.shape[2]), jnp.float32)
    for tap in range(9):
        above = tap // 3
        left = tap % 3
        window = padded[:, above:above + rows, left:left + cols, :].reshape(-1, chans)
        total = total + jnp.dot(window, kernel[tap], preferred_element_type=jnp.float32)
    return total.reshape(samples, rows, cols, kernel.shape[2])


def flipped(kernel):
    return jnp.transpose(kernel[::-1], (0, 2, 1))


def weight_terms(field, grad):
    samples, rows, cols, chans = field.shape
    padded = jnp.pad(field, ((0, 0), (1, 1), (1, 1), (0, 0)))
    grad_flat = grad.reshape(-1, grad.shape[3])
    terms = []
    for tap in range(9):
        above = tap // 3
        left = tap % 3
        window = padded[:, above:above + rows, left:left + cols, :].reshape(-1, chans)
        terms.append(lax.dot_general(window, grad_flat, (((0,), (0,)), ((), ())), preferred_element_type=jnp.float32))
    return jnp.stack(terms, 0)


def rounded(value):
    return lax.optimization_barrier(value.astype(jnp.bfloat16)).astype(jnp.float32)


def reference(inputs, cotangent, conv_first, conv_second):
    pre = conv_taps(inputs, conv_first)
    hidden = jax.nn.silu(pre).astype(jnp.bfloat16)
    outputs = (inputs.astype(jnp.float32) + conv_taps(hidden, conv_second)).astype(jnp.bfloat16)
    back = conv_taps(cotangent, flipped(conv_second))
    sigma = jax.nn.sigmoid(pre)
    dpre = (back * sigma * (1.0 + pre * (1.0 - sigma))).astype(jnp.bfloat16)
    blocks = SAMPLES // SAMP_DEV
    shape = (blocks, SAMP_DEV, HH, WW, C)

    def step(carry, pieces):
        block_in, block_dpre, block_hidden, block_cot = pieces
        first = rounded(weight_terms(block_in, block_dpre))
        second = rounded(weight_terms(block_hidden, block_cot))
        return (carry[0] + first, carry[1] + second), None

    start = (jnp.zeros((9, C, C), jnp.float32), jnp.zeros((9, C, C), jnp.float32))
    sums, unused = lax.scan(step, start, (inputs.reshape(shape), dpre.reshape(shape), hidden.reshape(shape), cotangent.reshape(shape)))
    grad_first = (sums[0] / SAMPLES).astype(jnp.bfloat16)
    grad_second = (sums[1] / SAMPLES).astype(jnp.bfloat16)
    return (outputs, grad_first, grad_second)
```

```python
import functools

import jax
import jax.numpy as jnp
from jax import lax
from jax.experimental import pallas as pl
from jax.experimental.pallas import tpu as pltpu
from jax.sharding import PartitionSpec as P

F32 = jnp.float32
BF16 = jnp.bfloat16
VMEM_LIMIT = 40 * 1024 * 1024


def column_shifted(field, cols, by):
    cells = field.shape[0]
    col = lax.broadcasted_iota(jnp.int32, field.shape, 0) % cols
    if by == 0:
        return field
    rolled = pltpu.roll(field, (-by) % cells, 0)
    return jnp.where(col == (cols - 1 if by > 0 else 0), 0.0, rolled)


def fill_taps(dst, field, cols, order):
    cells, chans = field.shape
    zeros = jnp.zeros((cols, dst.shape[1]), dst.dtype)
    dst[0:cols, :] = zeros
    dst[cols + cells : cols + cells + cols, :] = zeros
    for slot, by in enumerate(order):
        dst[cols : cols + cells, slot * chans : (slot + 1) * chans] = column_shifted(
            field, cols, by
        ).astype(dst.dtype)


def join_halves(dst, own, other, half, start, away):
    dst[:, pl.ds(start, half)] = own[...]
    dst[:, pl.ds(away, half)] = other[...]


def place(half):
    mine = lax.axis_index("shard")
    start = pl.multiple_of(mine * half, half)
    away = pl.multiple_of((1 - mine) * half, half)
    return start, away


def first_kernel(
    cols, x_own, x_other, c_own, c_other, w_own, w_other,
    grad_ref, hidden_ref, slope_ref,
    weight, taps, narrow, turned, pre_ref,
):
    cells, chans = x_own.shape
    half = w_own.shape[1]
    start, away = place(half)
    join_halves(weight, w_own, w_other, half, start, away)
    for sample, (x_ref, c_ref) in enumerate(((x_own, c_own), (x_other, c_other))):
        fill_taps(taps, x_ref[...].astype(F32), cols, (-1, 0, 1))
        pre = jnp.zeros((cells, chans), F32)
        for above in range(3):
            pre = pre + jnp.dot(
                taps[above * cols : above * cols + cells, :],
                weight[above * 3 * chans : (above + 1) * 3 * chans, :],
                preferred_element_type=F32,
            )
        pre_ref[...] = pre
        hidden = pre * jax.nn.sigmoid(pre)
        if sample == 0:
            hidden_ref[...] = hidden.astype(BF16)
        turned[:, sample * cells : (sample + 1) * cells] = hidden.T.astype(BF16)
        mine = pre_ref[:, pl.ds(start, half)]
        sg = jax.nn.sigmoid(mine)
        slope_ref[sample * cells : (sample + 1) * cells, :] = sg * (1.0 + mine * (1.0 - sg))
        fill_taps(narrow.at[sample], c_ref[:, pl.ds(start, half)].astype(F32), cols, (1, 0, -1))
    weight_grad(cols, turned, narrow, grad_ref)


def weight_grad(cols, turned, narrow, grad_ref):
    chans = turned.shape[0]
    half = grad_ref.shape[1]
    cells = turned.shape[1] // 2
    for above in range(3):
        at = (2 - above) * cols
        part = jnp.zeros((chans, 3 * half), F32)
        for sample in range(2):
            part = part + jnp.dot(
                turned[:, sample * cells : (sample + 1) * cells],
                narrow[sample, at : at + cells, :],
                preferred_element_type=F32,
            )
        for left in range(3):
            tap = 3 * above + left
            grad_ref[tap * chans : (tap + 1) * chans, :] = part[
                :, left * half : (left + 1) * half
            ].astype(BF16)


def second_kernel(
    cols, x_own, x_other, c_own, c_other, w_own, w_other, slope_ref,
    grad_ref,
    weight, taps, narrow, turned,
):
    cells, chans = x_own.shape
    half = w_own.shape[1]
    start, away = place(half)
    join_halves(weight, w_own, w_other, half, start, away)
    for sample, (x_ref, c_ref) in enumerate(((x_own, c_own), (x_other, c_other))):
        fill_taps(taps, c_ref[...].astype(F32), cols, (1, 0, -1))
        turned[:, sample * cells : (sample + 1) * cells] = x_ref[...].astype(F32).T.astype(BF16)
        back = jnp.zeros((cells, half), F32)
        for tap in range(9):
            above, left = tap // 3, tap % 3
            at = (2 - above) * cols
            back = back + lax.dot_general(
                taps[at : at + cells, left * chans : (left + 1) * chans],
                weight[pl.ds(pl.multiple_of(tap * chans + start, half), half), :],
                (((1,), (1,)), ((), ())),
                preferred_element_type=F32,
            )
        dpre = back * slope_ref[sample * cells : (sample + 1) * cells, :]
        fill_taps(narrow.at[sample], dpre, cols, (1, 0, -1))
    weight_grad(cols, turned, narrow, grad_ref)


def output_kernel(cols, x_ref, h_ref, w_own, w_other, out_ref, weight, taps):
    cells, chans = x_ref.shape
    half = w_own.shape[1]
    start, away = place(half)
    join_halves(weight, w_own, w_other, half, start, away)
    fill_taps(taps, h_ref[...].astype(F32), cols, (-1, 0, 1))
    total = x_ref[...].astype(F32)
    for above in range(3):
        total = total + jnp.dot(
            taps[above * cols : above * cols + cells, :],
            weight[above * 3 * chans : (above + 1) * 3 * chans, :],
            preferred_element_type=F32,
        )
    out_ref[...] = total.astype(BF16)


def call(kernel, cols, outs, scratch, flops, *args):
    moved = sum(a.size * a.dtype.itemsize for a in args)
    return pl.pallas_call(
        functools.partial(kernel, cols),
        out_shape=outs,
        in_specs=[pl.BlockSpec(memory_space=pltpu.VMEM)] * len(args),
        out_specs=jax.tree.map(lambda _: pl.BlockSpec(memory_space=pltpu.VMEM), outs),
        scratch_shapes=scratch,
        compiler_params=pltpu.CompilerParams(vmem_limit_bytes=VMEM_LIMIT),
        cost_estimate=pl.CostEstimate(flops=flops, bytes_accessed=moved, transcendentals=0),
    )(*args)


def cube_orders(bits):
    plain = list(range(bits))
    return plain, ([1, 0] + plain[2:] if bits > 2 else plain)


def cube_swap(value, orders, step):
    devices = lax.axis_size("dp")
    pairs = [
        (2 * d + c, 2 * (d ^ (1 << orders[c][step])) + c) for d in range(devices) for c in range(2)
    ]
    return lax.ppermute(value, ("dp", "shard"), pairs)


def cube_bit(orders, step):
    core = lax.axis_index("shard")
    return (lax.axis_index("dp") >> jnp.where(core == 0, orders[0][step], orders[1][step])) & 1


def summed_over_dp(value, scale):
    devices = lax.axis_size("dp")
    bits = devices.bit_length() - 1
    if devices != 1 << bits or bits == 0 or value.shape[0] % (1 << (bits - 1)):
        return (lax.psum(value.astype(F32), "dp") * scale).astype(BF16)
    orders = cube_orders(bits)
    for step in range(bits - 1):
        half = value.shape[0] // 2
        bit = cube_bit(orders, step)
        sent = lax.dynamic_slice_in_dim(value, (1 - bit) * half, half, 0)
        kept = lax.dynamic_slice_in_dim(value, bit * half, half, 0)
        came = cube_swap(sent, orders, step)
        value = (kept.astype(F32) + came.astype(F32)).astype(BF16)
    came = cube_swap(value, orders, bits - 1)
    value = ((value.astype(F32) + came.astype(F32)) * scale).astype(BF16)
    for step in range(bits - 2, -1, -1):
        came = cube_swap(value, orders, step)
        bit = cube_bit(orders, step)
        value = jnp.where(
            bit == 0,
            jnp.concatenate([value, came], 0),
            jnp.concatenate([came, value], 0),
        )
    return value


def body(inputs, cotangent, conv_first, conv_second):
    _, rows, cols, chans = inputs.shape
    cells = rows * cols
    half = conv_first.shape[2]
    swap = [(0, 1), (1, 0)]
    x_own = inputs.reshape(cells, chans)
    c_own = cotangent.reshape(cells, chans)
    w1_own = conv_first.reshape(9 * chans, half)
    w2_own = conv_second.reshape(9 * chans, half)
    w1_other, x_other, c_other, w2_other = (
        lax.ppermute(v, "shard", swap) for v in (w1_own, x_own, c_own, w2_own)
    )
    unit = 2 * 9 * cells * chans * chans
    weight = pltpu.VMEM((9 * chans, chans), BF16)
    taps = pltpu.VMEM((cells + 2 * cols, 3 * chans), BF16)
    narrow = pltpu.VMEM((2, cells + 2 * cols, 3 * half), BF16)
    turned = pltpu.VMEM((chans, 2 * cells), BF16)
    grad_shape = jax.ShapeDtypeStruct((9 * chans, half), BF16)
    second, hidden, slope = call(
        first_kernel,
        cols,
        (
            grad_shape,
            jax.ShapeDtypeStruct((cells, chans), BF16),
            jax.ShapeDtypeStruct((2 * cells, half), F32),
        ),
        [weight, taps, narrow, turned, pltpu.VMEM((cells, chans), F32)],
        3 * unit,
        x_own, x_other, c_own, c_other, w1_own, w1_other,
    )
    first = call(
        second_kernel,
        cols,
        grad_shape,
        [weight, taps, narrow, turned],
        2 * unit,
        x_own, x_other, c_own, c_other, w2_own, w2_other, slope,
    )
    outputs = call(
        output_kernel,
        cols,
        jax.ShapeDtypeStruct((cells, chans), BF16),
        [weight, taps],
        unit,
        x_own, hidden, w2_own, w2_other,
    )
    scale = 1.0 / (inputs.shape[0] * lax.axis_size("dp") * lax.axis_size("shard"))
    grad_second = summed_over_dp(second, scale)
    grad_first = summed_over_dp(first, scale)
    return (
        outputs.reshape(inputs.shape),
        grad_first.reshape(conv_first.shape),
        grad_second.reshape(conv_second.shape),
    )


def solution(mesh):
    placed = (
        P(("group", "dp", "shard"), None, None, None),
        P(("group", "dp", "shard"), None, None, None),
        P("group", None, "shard"),
        P("group", None, "shard"),
    )
    return jax.shard_map(
        body,
        mesh=mesh,
        in_specs=placed,
        out_specs=(
            P(("group", "dp", "shard"), None, None, None),
            P("group", None, "shard"),
            P("group", None, "shard"),
        ),
        check_vma=False,
    )
```

```python
import functools

import jax
import jax.numpy as jnp
from jax import lax
from jax.experimental import pallas as pl
from jax.experimental.pallas import tpu as pltpu
from jax.sharding import PartitionSpec as P

F32 = jnp.float32
BF16 = jnp.bfloat16
DEPS = {(1, 2): (2,)}
VMEM_LIMIT = 16 * 1024 * 1024


def column_shifted(field, cols, by):
    cells = field.shape[0]
    col = lax.broadcasted_iota(jnp.int32, field.shape, 0) % cols
    if by == 0:
        return field
    rolled = pltpu.roll(field, (-by) % cells, 0)
    return jnp.where(col == (cols - 1 if by > 0 else 0), 0.0, rolled)


def fill_taps(dst, field, cols, order):
    cells, chans = field.shape
    zeros = jnp.zeros((cols, dst.shape[1]), dst.dtype)
    dst[0:cols, :] = zeros
    dst[cols + cells : cols + cells + cols, :] = zeros
    for slot, by in enumerate(order):
        dst[cols : cols + cells, slot * chans : (slot + 1) * chans] = column_shifted(
            field, cols, by
        ).astype(dst.dtype)


def join_halves(dst, own, other, half, start, away):
    dst[:, pl.ds(start, half)] = own[...]
    dst[:, pl.ds(away, half)] = other[...]


def place(half):
    mine = lax.axis_index("shard")
    start = pl.multiple_of(mine * half, half)
    away = pl.multiple_of((1 - mine) * half, half)
    return start, away


def first_kernel(
    cols, x_own, x_other, c_own, c_other, w_own, w_other, ready_ref,
    grad_ref, hidden_ref, slope_ref,
    weight, taps, narrow, turned, pre_ref,
):
    cells, chans = x_own.shape
    half = w_own.shape[1]
    start, away = place(half)
    join_halves(weight, w_own, w_other, half, start, away)
    for sample, (x_ref, c_ref) in enumerate(((x_own, c_own), (x_other, c_other))):
        fill_taps(taps, x_ref[...].astype(F32), cols, (-1, 0, 1))
        pre = jnp.zeros((cells, chans), F32)
        for above in range(3):
            pre = pre + jnp.dot(
                taps[above * cols : above * cols + cells, :],
                weight[above * 3 * chans : (above + 1) * 3 * chans, :],
                preferred_element_type=F32,
            )
        pre_ref[...] = pre
        hidden = pre * jax.nn.sigmoid(pre)
        if sample == 0:
            hidden_ref[...] = hidden.astype(BF16)
        turned[:, sample * cells : (sample + 1) * cells] = hidden.T.astype(BF16)
        mine = pre_ref[:, pl.ds(start, half)]
        sg = jax.nn.sigmoid(mine)
        slope_ref[sample * cells : (sample + 1) * cells, :] = sg * (1.0 + mine * (1.0 - sg))
        fill_taps(narrow.at[sample], c_ref[:, pl.ds(start, half)].astype(F32), cols, (1, 0, -1))
    weight_grad(cols, turned, narrow, grad_ref)


def ready_kernel(cols, out_ref):
    out_ref[...] = jnp.zeros(out_ref.shape, F32)


def weight_grad(cols, turned, narrow, grad_ref):
    chans = turned.shape[0]
    half = grad_ref.shape[1]
    cells = turned.shape[1] // 2
    for above in range(3):
        at = (2 - above) * cols
        part = jnp.zeros((chans, 3 * half), F32)
        for sample in range(2):
            part = part + jnp.dot(
                turned[:, sample * cells : (sample + 1) * cells],
                narrow[sample, at : at + cells, :],
                preferred_element_type=F32,
            )
        for left in range(3):
            tap = 3 * above + left
            grad_ref[tap * chans : (tap + 1) * chans, :] = part[
                :, left * half : (left + 1) * half
            ].astype(BF16)


def second_kernel(
    cols, x_own, x_other, c_own, c_other, w_own, w_other, slope_ref,
    grad_ref,
    weight, taps, narrow, turned,
):
    cells, chans = x_own.shape
    half = w_own.shape[1]
    start, away = place(half)
    join_halves(weight, w_own, w_other, half, start, away)
    for sample, (x_ref, c_ref) in enumerate(((x_own, c_own), (x_other, c_other))):
        fill_taps(taps, c_ref[...].astype(F32), cols, (1, 0, -1))
        turned[:, sample * cells : (sample + 1) * cells] = x_ref[...].astype(F32).T.astype(BF16)
        back = jnp.zeros((cells, half), F32)
        for tap in range(9):
            above, left = tap // 3, tap % 3
            at = (2 - above) * cols
            back = back + lax.dot_general(
                taps[at : at + cells, left * chans : (left + 1) * chans],
                weight[pl.ds(pl.multiple_of(tap * chans + start, half), half), :],
                (((1,), (1,)), ((), ())),
                preferred_element_type=F32,
            )
        dpre = back * slope_ref[sample * cells : (sample + 1) * cells, :]
        fill_taps(narrow.at[sample], dpre, cols, (1, 0, -1))
    weight_grad(cols, turned, narrow, grad_ref)


def output_kernel(cols, x_ref, h_ref, w_own, w_other, out_ref, weight, taps):
    cells, chans = x_ref.shape
    half = w_own.shape[1]
    start, away = place(half)
    join_halves(weight, w_own, w_other, half, start, away)
    fill_taps(taps, h_ref[...].astype(F32), cols, (-1, 0, 1))
    total = x_ref[...].astype(F32)
    for above in range(3):
        total = total + jnp.dot(
            taps[above * cols : above * cols + cells, :],
            weight[above * 3 * chans : (above + 1) * 3 * chans, :],
            preferred_element_type=F32,
        )
    out_ref[...] = total.astype(BF16)


def call(kernel, cols, outs, scratch, flops, *args):
    moved = sum(a.size * a.dtype.itemsize for a in args)
    return pl.pallas_call(
        functools.partial(kernel, cols),
        out_shape=outs,
        in_specs=[pl.BlockSpec(memory_space=pltpu.VMEM)] * len(args),
        out_specs=jax.tree.map(lambda _: pl.BlockSpec(memory_space=pltpu.VMEM), outs),
        scratch_shapes=scratch,
        compiler_params=pltpu.CompilerParams(vmem_limit_bytes=VMEM_LIMIT),
        cost_estimate=pl.CostEstimate(flops=flops, bytes_accessed=moved, transcendentals=0),
    )(*args)


def cube_orders(bits):
    plain = list(range(bits))
    return plain, ([1, 0] + plain[2:] if bits > 2 else plain)


def cube_swap(value, orders, step):
    devices = lax.axis_size("dp")
    pairs = [
        (2 * d + c, 2 * (d ^ (1 << orders[c][step])) + c) for d in range(devices) for c in range(2)
    ]
    return lax.ppermute(value, ("dp", "shard"), pairs)


def cube_bit(orders, step):
    core = lax.axis_index("shard")
    return (lax.axis_index("dp") >> jnp.where(core == 0, orders[0][step], orders[1][step])) & 1


def cube_halves(value, orders, step):
    half = value.shape[0] // 2
    bit = cube_bit(orders, step)
    sent = lax.dynamic_slice_in_dim(value, (1 - bit) * half, half, 0)
    kept = lax.dynamic_slice_in_dim(value, bit * half, half, 0)
    return sent, kept


def added(kept, came):
    return (kept.astype(F32) + came.astype(F32)).astype(BF16)


def after(value, *others):
    return lax.optimization_barrier((value, *others))[0]


def summed_over_dp(early, make_late, scale, outputs):
    devices = lax.axis_size("dp")
    bits = devices.bit_length() - 1
    orders = cube_orders(bits)
    last = bits - 1
    steps = list(range(bits)) + list(range(bits - 2, -1, -1))
    values = [early, None]
    came = [{}, {}]

    def send(which, k):
        step = steps[k]
        value = values[which]
        if k < last:
            sent, _ = cube_halves(value, orders, step)
        else:
            sent = value
        for other in DEPS.get((which, k), ()):
            if other == "out":
                sent = after(sent, outputs)
            elif other in came[1 - which]:
                sent = after(sent, came[1 - which][other])
        came[which][k] = cube_swap(sent, orders, step)

    def take(which, k):
        step = steps[k]
        value, got = values[which], came[which][k]
        if k < last:
            value = added(cube_halves(value, orders, step)[1], got)
        elif k == last:
            value = ((value.astype(F32) + got.astype(F32)) * scale).astype(BF16)
        else:
            bit = cube_bit(orders, step)
            value = jnp.where(
                bit == 0,
                jnp.concatenate([value, got], 0),
                jnp.concatenate([got, value], 0),
            )
        values[which] = value

    send(0, 0)
    values[1] = make_late()
    for k in range(len(steps)):
        send(1, k) if k == 0 else None
        take(0, k)
        if k + 1 < len(steps):
            send(0, k + 1)
        if k >= 1:
            take(1, k - 1)
            send(1, k)
    take(1, len(steps) - 1)
    return values


def body(inputs, cotangent, conv_first, conv_second):
    _, rows, cols, chans = inputs.shape
    cells = rows * cols
    half = conv_first.shape[2]
    swap = [(0, 1), (1, 0)]
    x_own = inputs.reshape(cells, chans)
    c_own = cotangent.reshape(cells, chans)
    w1_own = conv_first.reshape(9 * chans, half)
    w2_own = conv_second.reshape(9 * chans, half)
    w1_other, x_other, c_other, w2_other = (
        lax.ppermute(v, "shard", swap) for v in (w1_own, x_own, c_own, w2_own)
    )
    unit = 2 * 9 * cells * chans * chans
    weight = pltpu.VMEM((9 * chans, chans), BF16)
    taps = pltpu.VMEM((cells + 2 * cols, 3 * chans), BF16)
    narrow = pltpu.VMEM((2, cells + 2 * cols, 3 * half), BF16)
    turned = pltpu.VMEM((chans, 2 * cells), BF16)
    grad_shape = jax.ShapeDtypeStruct((9 * chans, half), BF16)
    ready = call(ready_kernel, cols, jax.ShapeDtypeStruct((8, 128), F32), [], 4 * unit)
    second, hidden, slope = call(
        first_kernel,
        cols,
        (
            grad_shape,
            jax.ShapeDtypeStruct((cells, chans), BF16),
            jax.ShapeDtypeStruct((2 * cells, half), F32),
        ),
        [weight, taps, narrow, turned, pltpu.VMEM((cells, chans), F32)],
        3 * unit,
        x_own, x_other, c_own, c_other, w1_own, w1_other, ready,
    )
    def make_late():
        return call(
            second_kernel,
            cols,
            grad_shape,
            [weight, taps, narrow, turned],
            2 * unit,
            x_own, x_other, c_own, c_other, w2_own, w2_other, slope,
        )

    outputs = call(
        output_kernel,
        cols,
        jax.ShapeDtypeStruct((cells, chans), BF16),
        [weight, taps],
        unit,
        x_own, hidden, w2_own, w2_other,
    )
    scale = 1.0 / (inputs.shape[0] * lax.axis_size("dp") * lax.axis_size("shard"))
    grad_second, grad_first = summed_over_dp(second, make_late, scale, outputs)
    return (
        outputs.reshape(inputs.shape),
        grad_first.reshape(conv_first.shape),
        grad_second.reshape(conv_second.shape),
    )


def solution(mesh):
    placed = (
        P(("group", "dp", "shard"), None, None, None),
        P(("group", "dp", "shard"), None, None, None),
        P("group", None, "shard"),
        P("group", None, "shard"),
    )
    return jax.shard_map(
        body,
        mesh=mesh,
        in_specs=placed,
        out_specs=(
            P(("group", "dp", "shard"), None, None, None),
            P("group", None, "shard"),
            P("group", None, "shard"),
        ),
        check_vma=False,
    )
```

```python
import functools

import jax
import jax.numpy as jnp
from jax import lax
from jax.experimental import pallas as pl
from jax.experimental.pallas import tpu as pltpu
from jax.sharding import PartitionSpec as P

F32 = jnp.float32
BF16 = jnp.bfloat16
VMEM_LIMIT = 16 * 1024 * 1024


def column_shifted(field, cols, by):
    cells = field.shape[0]
    col = lax.broadcasted_iota(jnp.int32, field.shape, 0) % cols
    if by == 0:
        return field
    rolled = pltpu.roll(field, (-by) % cells, 0)
    return jnp.where(col == (cols - 1 if by > 0 else 0), 0.0, rolled)


def fill_taps(dst, field, cols, order):
    cells, chans = field.shape
    zeros = jnp.zeros((cols, dst.shape[1]), dst.dtype)
    dst[0:cols, :] = zeros
    dst[cols + cells : cols + cells + cols, :] = zeros
    for slot, by in enumerate(order):
        dst[cols : cols + cells, slot * chans : (slot + 1) * chans] = column_shifted(
            field, cols, by
        ).astype(dst.dtype)


def join_halves(dst, own, other, half, start, away):
    dst[:, pl.ds(start, half)] = own[...]
    dst[:, pl.ds(away, half)] = other[...]


def place(half):
    mine = lax.axis_index("shard")
    start = pl.multiple_of(mine * half, half)
    away = pl.multiple_of((1 - mine) * half, half)
    return start, away


def first_kernel(
    cols, x_own, x_other, c_own, c_other, w_own, w_other, ready_ref,
    grad_ref, hidden_ref, slope_ref,
    weight, taps, narrow, turned, pre_ref,
):
    cells, chans = x_own.shape
    half = w_own.shape[1]
    start, away = place(half)
    join_halves(weight, w_own, w_other, half, start, away)
    for sample, (x_ref, c_ref) in enumerate(((x_own, c_own), (x_other, c_other))):
        fill_taps(taps, x_ref[...].astype(F32), cols, (-1, 0, 1))
        pre = jnp.zeros((cells, chans), F32)
        for above in range(3):
            pre = pre + jnp.dot(
                taps[above * cols : above * cols + cells, :],
                weight[above * 3 * chans : (above + 1) * 3 * chans, :],
                preferred_element_type=F32,
            )
        pre_ref[...] = pre
        hidden = pre * jax.nn.sigmoid(pre)
        if sample == 0:
            hidden_ref[...] = hidden.astype(BF16)
        turned[:, sample * cells : (sample + 1) * cells] = hidden.T.astype(BF16)
        mine = pre_ref[:, pl.ds(start, half)]
        sg = jax.nn.sigmoid(mine)
        slope_ref[sample * cells : (sample + 1) * cells, :] = sg * (1.0 + mine * (1.0 - sg))
        fill_taps(narrow.at[sample], c_ref[:, pl.ds(start, half)].astype(F32), cols, (1, 0, -1))
    weight_grad(cols, turned, narrow, grad_ref)


def ready_kernel(cols, out_ref):
    out_ref[...] = jnp.zeros(out_ref.shape, F32)


def weight_grad(cols, turned, narrow, grad_ref):
    chans = turned.shape[0]
    half = grad_ref.shape[1]
    cells = turned.shape[1] // 2
    for above in range(3):
        at = (2 - above) * cols
        part = jnp.zeros((chans, 3 * half), F32)
        for sample in range(2):
            part = part + jnp.dot(
                turned[:, sample * cells : (sample + 1) * cells],
                narrow[sample, at : at + cells, :],
                preferred_element_type=F32,
            )
        for left in range(3):
            tap = 3 * above + left
            grad_ref[tap * chans : (tap + 1) * chans, :] = part[
                :, left * half : (left + 1) * half
            ].astype(BF16)


def second_kernel(
    cols, x_own, x_other, c_own, c_other, w_own, w_other, slope_ref,
    grad_ref,
    weight, taps, narrow, turned,
):
    cells, chans = x_own.shape
    half = w_own.shape[1]
    start, away = place(half)
    join_halves(weight, w_own, w_other, half, start, away)
    for sample, (x_ref, c_ref) in enumerate(((x_own, c_own), (x_other, c_other))):
        fill_taps(taps, c_ref[...].astype(F32), cols, (1, 0, -1))
        turned[:, sample * cells : (sample + 1) * cells] = x_ref[...].astype(F32).T.astype(BF16)
        back = jnp.zeros((cells, half), F32)
        for tap in range(9):
            above, left = tap // 3, tap % 3
            at = (2 - above) * cols
            back = back + lax.dot_general(
                taps[at : at + cells, left * chans : (left + 1) * chans],
                weight[pl.ds(pl.multiple_of(tap * chans + start, half), half), :],
                (((1,), (1,)), ((), ())),
                preferred_element_type=F32,
            )
        dpre = back * slope_ref[sample * cells : (sample + 1) * cells, :]
        fill_taps(narrow.at[sample], dpre, cols, (1, 0, -1))
    weight_grad(cols, turned, narrow, grad_ref)


def output_kernel(cols, x_ref, h_ref, w_own, w_other, out_ref, weight, taps):
    cells, chans = x_ref.shape
    half = w_own.shape[1]
    start, away = place(half)
    join_halves(weight, w_own, w_other, half, start, away)
    fill_taps(taps, h_ref[...].astype(F32), cols, (-1, 0, 1))
    total = x_ref[...].astype(F32)
    for above in range(3):
        total = total + jnp.dot(
            taps[above * cols : above * cols + cells, :],
            weight[above * 3 * chans : (above + 1) * 3 * chans, :],
            preferred_element_type=F32,
        )
    out_ref[...] = total.astype(BF16)


def call(kernel, cols, outs, scratch, flops, *args):
    moved = sum(a.size * a.dtype.itemsize for a in args)
    return pl.pallas_call(
        functools.partial(kernel, cols),
        out_shape=outs,
        in_specs=[pl.BlockSpec(memory_space=pltpu.VMEM)] * len(args),
        out_specs=jax.tree.map(lambda _: pl.BlockSpec(memory_space=pltpu.VMEM), outs),
        scratch_shapes=scratch,
        compiler_params=pltpu.CompilerParams(vmem_limit_bytes=VMEM_LIMIT),
        cost_estimate=pl.CostEstimate(flops=flops, bytes_accessed=moved, transcendentals=0),
    )(*args)


def swapped(value, mask):
    pairs = [(d, d ^ mask) for d in range(lax.axis_size("dp"))]
    return lax.ppermute(value, "dp", pairs)


def after(value, *others):
    return lax.optimization_barrier((value, *others))[0]


class Summed:
    def __init__(self, value, scale):
        devices = lax.axis_size("dp")
        bits = devices.bit_length() - 1
        assert devices == 1 << bits
        self.near = min(4, devices)
        self.far = [1 << k for k in range(self.near.bit_length() - 1, bits)]
        self.rows = value.shape[0] // self.near
        self.value, self.scale = value, scale
        self.at = lax.axis_index("dp") % self.near

    def quarter(self, index):
        return lax.dynamic_slice_in_dim(self.value, index * self.rows, self.rows, 0)

    def scatter(self):
        sent = [self.quarter(self.at ^ mask) for mask in range(1, self.near)]
        self.came = [swapped(v, mask + 1) for mask, v in enumerate(sent)]

    def add(self):
        total = self.quarter(self.at).astype(F32)
        for came in self.came:
            total = total + came.astype(F32)
        self.sum = total if not self.far else total.astype(BF16)

    def swap(self, *others):
        for k, mask in enumerate(self.far):
            sent = after(self.sum, *others) if k == 0 and others else self.sum
            self.came = [swapped(sent, mask)]
            if k + 1 < len(self.far):
                self.sum = (self.sum.astype(F32) + self.came[0].astype(F32)).astype(BF16)

    def finish(self):
        total = self.sum.astype(F32)
        if self.far:
            total = total + self.came[0].astype(F32)
        self.sum = (total * self.scale).astype(BF16)

    def gather(self, *others):
        sent = after(self.sum, *others) if others else self.sum
        self.came = [swapped(sent, mask) for mask in range(1, self.near)]

    def result(self):
        whole = jnp.zeros(self.value.shape, BF16)
        for mask, piece in enumerate([self.sum] + self.came):
            whole = lax.dynamic_update_slice_in_dim(whole, piece, (self.at ^ mask) * self.rows, 0)
        return whole


def body(inputs, cotangent, conv_first, conv_second):
    _, rows, cols, chans = inputs.shape
    cells = rows * cols
    half = conv_first.shape[2]
    swap = [(0, 1), (1, 0)]
    x_own = inputs.reshape(cells, chans)
    c_own = cotangent.reshape(cells, chans)
    w1_own = conv_first.reshape(9 * chans, half)
    w2_own = conv_second.reshape(9 * chans, half)
    w1_other, x_other, c_other, w2_other = (
        lax.ppermute(v, "shard", swap) for v in (w1_own, x_own, c_own, w2_own)
    )
    unit = 2 * 9 * cells * chans * chans
    weight = pltpu.VMEM((9 * chans, chans), BF16)
    taps = pltpu.VMEM((cells + 2 * cols, 3 * chans), BF16)
    narrow = pltpu.VMEM((2, cells + 2 * cols, 3 * half), BF16)
    turned = pltpu.VMEM((chans, 2 * cells), BF16)
    grad_shape = jax.ShapeDtypeStruct((9 * chans, half), BF16)
    ready = call(ready_kernel, cols, jax.ShapeDtypeStruct((8, 128), F32), [], 4 * unit)
    second, hidden, slope = call(
        first_kernel,
        cols,
        (
            grad_shape,
            jax.ShapeDtypeStruct((cells, chans), BF16),
            jax.ShapeDtypeStruct((2 * cells, half), F32),
        ),
        [weight, taps, narrow, turned, pltpu.VMEM((cells, chans), F32)],
        3 * unit,
        x_own, x_other, c_own, c_other, w1_own, w1_other, ready,
    )
    def make_late():
        return call(
            second_kernel,
            cols,
            grad_shape,
            [weight, taps, narrow, turned],
            2 * unit,
            x_own, x_other, c_own, c_other, w2_own, w2_other, slope,
        )

    outputs = call(
        output_kernel,
        cols,
        jax.ShapeDtypeStruct((cells, chans), BF16),
        [weight, taps],
        unit,
        x_own, hidden, w2_own, w2_other,
    )
    scale = 1.0 / (inputs.shape[0] * lax.axis_size("dp") * lax.axis_size("shard"))
    early, late = Summed(second, scale), None
    early.scatter()
    late = Summed(make_late(), scale)
    late.scatter()
    early.add()
    early.swap()
    late.add()
    late.swap()
    early.finish()
    early.gather()
    late.finish()
    late.gather()
    grad_second, grad_first = early.result(), late.result()
    return (
        outputs.reshape(inputs.shape),
        grad_first.reshape(conv_first.shape),
        grad_second.reshape(conv_second.shape),
    )


def solution(mesh):
    placed = (
        P(("group", "dp", "shard"), None, None, None),
        P(("group", "dp", "shard"), None, None, None),
        P("group", None, "shard"),
        P("group", None, "shard"),
    )
    return jax.shard_map(
        body,
        mesh=mesh,
        in_specs=placed,
        out_specs=(
            P(("group", "dp", "shard"), None, None, None),
            P("group", None, "shard"),
            P("group", None, "shard"),
        ),
        check_vma=False,
    )
```

```python
import functools

import jax
import jax.numpy as jnp
from jax import lax
from jax.experimental import pallas as pl
from jax.experimental.pallas import tpu as pltpu
from jax.sharding import PartitionSpec as P

F32 = jnp.float32
BF16 = jnp.bfloat16
VMEM_LIMIT = 16 * 1024 * 1024


def column_shifted(field, cols, by):
    cells = field.shape[0]
    col = lax.broadcasted_iota(jnp.int32, field.shape, 0) % cols
    if by == 0:
        return field
    rolled = pltpu.roll(field, (-by) % cells, 0)
    return jnp.where(col == (cols - 1 if by > 0 else 0), 0.0, rolled)


def fill_taps(dst, field, cols, order):
    cells, chans = field.shape
    zeros = jnp.zeros((cols, dst.shape[1]), dst.dtype)
    dst[0:cols, :] = zeros
    dst[cols + cells : cols + cells + cols, :] = zeros
    for slot, by in enumerate(order):
        dst[cols : cols + cells, slot * chans : (slot + 1) * chans] = column_shifted(
            field, cols, by
        ).astype(dst.dtype)


def join_halves(dst, own, other, half, start, away):
    dst[:, pl.ds(start, half)] = own[...]
    dst[:, pl.ds(away, half)] = other[...]


def place(half):
    mine = lax.axis_index("shard")
    start = pl.multiple_of(mine * half, half)
    away = pl.multiple_of((1 - mine) * half, half)
    return start, away


def first_kernel(
    cols, x_own, x_other, c_own, c_other, w_own, w_other, ready_ref,
    grad_ref, hidden_ref, slope_ref,
    weight, taps, narrow, turned, pre_ref, sg_ref,
):
    cells, chans = x_own.shape
    half = w_own.shape[1]
    start, away = place(half)
    join_halves(weight, w_own, w_other, half, start, away)
    for sample, (x_ref, c_ref) in enumerate(((x_own, c_own), (x_other, c_other))):
        fill_taps(taps, x_ref[...].astype(F32), cols, (-1, 0, 1))
        pre = jnp.zeros((cells, chans), F32)
        for above in range(3):
            pre = pre + jnp.dot(
                taps[above * cols : above * cols + cells, :],
                weight[above * 3 * chans : (above + 1) * 3 * chans, :],
                preferred_element_type=F32,
            )
        pre_ref[...] = pre
        sg_all = jax.nn.sigmoid(pre)
        sg_ref[...] = sg_all
        hidden = pre * sg_all
        if sample == 0:
            hidden_ref[...] = hidden.astype(BF16)
        turned[:, sample * cells : (sample + 1) * cells] = hidden.astype(BF16).T
        mine = pre_ref[:, pl.ds(start, half)]
        sg = sg_ref[:, pl.ds(start, half)]
        slope_ref[sample * cells : (sample + 1) * cells, :] = sg * (1.0 + mine * (1.0 - sg))
        fill_taps(narrow.at[sample], c_ref[:, pl.ds(start, half)].astype(F32), cols, (1, 0, -1))
    weight_grad(cols, turned, narrow, grad_ref)


def ready_kernel(cols, out_ref):
    out_ref[...] = jnp.zeros(out_ref.shape, F32)


def weight_grad(cols, turned, narrow, grad_ref):
    chans = turned.shape[0]
    half = grad_ref.shape[1]
    cells = turned.shape[1] // 2
    for above in range(3):
        at = (2 - above) * cols
        part = jnp.zeros((chans, 3 * half), F32)
        for sample in range(2):
            part = part + jnp.dot(
                turned[:, sample * cells : (sample + 1) * cells],
                narrow[sample, at : at + cells, :],
                preferred_element_type=F32,
            )
        for left in range(3):
            tap = 3 * above + left
            grad_ref[tap * chans : (tap + 1) * chans, :] = part[
                :, left * half : (left + 1) * half
            ].astype(BF16)


def second_kernel(
    cols, x_own, x_other, c_own, c_other, w_own, w_other, slope_ref,
    grad_ref,
    weight, taps, narrow, turned,
):
    cells, chans = x_own.shape
    half = w_own.shape[1]
    start, away = place(half)
    join_halves(weight, w_own, w_other, half, start, away)
    for sample, (x_ref, c_ref) in enumerate(((x_own, c_own), (x_other, c_other))):
        fill_taps(taps, c_ref[...].astype(F32), cols, (1, 0, -1))
        turned[:, sample * cells : (sample + 1) * cells] = x_ref[...].astype(F32).T.astype(BF16)
        back = jnp.zeros((cells, half), F32)
        for tap in range(9):
            above, left = tap // 3, tap % 3
            at = (2 - above) * cols
            back = back + lax.dot_general(
                taps[at : at + cells, left * chans : (left + 1) * chans],
                weight[pl.ds(pl.multiple_of(tap * chans + start, half), half), :],
                (((1,), (1,)), ((), ())),
                preferred_element_type=F32,
            )
        dpre = back * slope_ref[sample * cells : (sample + 1) * cells, :]
        fill_taps(narrow.at[sample], dpre, cols, (1, 0, -1))
    weight_grad(cols, turned, narrow, grad_ref)


def output_kernel(cols, x_ref, h_ref, w_own, w_other, out_ref, weight, taps):
    cells, chans = x_ref.shape
    half = w_own.shape[1]
    start, away = place(half)
    join_halves(weight, w_own, w_other, half, start, away)
    fill_taps(taps, h_ref[...].astype(F32), cols, (-1, 0, 1))
    total = x_ref[...].astype(F32)
    for above in range(3):
        total = total + jnp.dot(
            taps[above * cols : above * cols + cells, :],
            weight[above * 3 * chans : (above + 1) * 3 * chans, :],
            preferred_element_type=F32,
        )
    out_ref[...] = total.astype(BF16)


def call(kernel, cols, outs, scratch, flops, *args):
    moved = sum(a.size * a.dtype.itemsize for a in args)
    return pl.pallas_call(
        functools.partial(kernel, cols),
        out_shape=outs,
        in_specs=[pl.BlockSpec(memory_space=pltpu.VMEM)] * len(args),
        out_specs=jax.tree.map(lambda _: pl.BlockSpec(memory_space=pltpu.VMEM), outs),
        scratch_shapes=scratch,
        compiler_params=pltpu.CompilerParams(vmem_limit_bytes=VMEM_LIMIT),
        cost_estimate=pl.CostEstimate(flops=flops, bytes_accessed=moved, transcendentals=0),
    )(*args)


def swapped(value, mask):
    pairs = [(d, d ^ mask) for d in range(lax.axis_size("dp"))]
    return lax.ppermute(value, "dp", pairs)


def after(value, *others):
    return lax.optimization_barrier((value, *others))[0]


class Summed:
    def __init__(self, value, scale):
        devices = lax.axis_size("dp")
        bits = devices.bit_length() - 1
        assert devices == 1 << bits
        self.near = min(4, devices)
        self.far = [1 << k for k in range(self.near.bit_length() - 1, bits)]
        self.rows = value.shape[0] // self.near
        self.value, self.scale = value, scale
        self.at = lax.axis_index("dp") % self.near

    def quarter(self, index):
        return lax.dynamic_slice_in_dim(self.value, index * self.rows, self.rows, 0)

    def scatter(self):
        sent = [self.quarter(self.at ^ mask) for mask in range(1, self.near)]
        self.came = [swapped(v, mask + 1) for mask, v in enumerate(sent)]

    def add(self):
        total = self.quarter(self.at).astype(F32)
        for came in self.came:
            total = total + came.astype(F32)
        self.sum = total if not self.far else total.astype(BF16)

    def swap(self, *others):
        for k, mask in enumerate(self.far):
            sent = after(self.sum, *others) if k == 0 and others else self.sum
            self.came = [swapped(sent, mask)]
            if k + 1 < len(self.far):
                self.sum = (self.sum.astype(F32) + self.came[0].astype(F32)).astype(BF16)

    def finish(self):
        total = self.sum.astype(F32)
        if self.far:
            total = total + self.came[0].astype(F32)
        self.sum = (total * self.scale).astype(BF16)

    def gather(self, *others):
        sent = after(self.sum, *others) if others else self.sum
        self.came = [swapped(sent, mask) for mask in range(1, self.near)]

    def result(self):
        whole = jnp.zeros(self.value.shape, BF16)
        for mask, piece in enumerate([self.sum] + self.came):
            whole = lax.dynamic_update_slice_in_dim(whole, piece, (self.at ^ mask) * self.rows, 0)
        return whole


def body(inputs, cotangent, conv_first, conv_second):
    _, rows, cols, chans = inputs.shape
    cells = rows * cols
    half = conv_first.shape[2]
    swap = [(0, 1), (1, 0)]
    x_own = inputs.reshape(cells, chans)
    c_own = cotangent.reshape(cells, chans)
    w1_own = conv_first.reshape(9 * chans, half)
    w2_own = conv_second.reshape(9 * chans, half)
    w1_other, x_other, c_other, w2_other = (
        lax.ppermute(v, "shard", swap) for v in (w1_own, x_own, c_own, w2_own)
    )
    unit = 2 * 9 * cells * chans * chans
    weight = pltpu.VMEM((9 * chans, chans), BF16)
    taps = pltpu.VMEM((cells + 2 * cols, 3 * chans), BF16)
    narrow = pltpu.VMEM((2, cells + 2 * cols, 3 * half), BF16)
    turned = pltpu.VMEM((chans, 2 * cells), BF16)
    grad_shape = jax.ShapeDtypeStruct((9 * chans, half), BF16)
    ready = call(ready_kernel, cols, jax.ShapeDtypeStruct((8, 128), F32), [], 4 * unit)
    second, hidden, slope = call(
        first_kernel,
        cols,
        (
            grad_shape,
            jax.ShapeDtypeStruct((cells, chans), BF16),
            jax.ShapeDtypeStruct((2 * cells, half), F32),
        ),
        [weight, taps, narrow, turned, pltpu.VMEM((cells, chans), F32), pltpu.VMEM((cells, chans), F32)],
        3 * unit,
        x_own, x_other, c_own, c_other, w1_own, w1_other, ready,
    )
    def make_late():
        return call(
            second_kernel,
            cols,
            grad_shape,
            [weight, taps, narrow, turned],
            2 * unit,
            x_own, x_other, c_own, c_other, w2_own, w2_other, slope,
        )

    outputs = call(
        output_kernel,
        cols,
        jax.ShapeDtypeStruct((cells, chans), BF16),
        [weight, taps],
        unit,
        x_own, hidden, w2_own, w2_other,
    )
    scale = 1.0 / (inputs.shape[0] * lax.axis_size("dp") * lax.axis_size("shard"))
    early, late = Summed(second, scale), None
    early.scatter()
    late = Summed(make_late(), scale)
    late.scatter()
    early.add()
    early.swap()
    late.add()
    late.swap()
    early.finish()
    early.gather()
    late.finish()
    late.gather()
    grad_second, grad_first = early.result(), late.result()
    return (
        outputs.reshape(inputs.shape),
        grad_first.reshape(conv_first.shape),
        grad_second.reshape(conv_second.shape),
    )


def solution(mesh):
    placed = (
        P(("group", "dp", "shard"), None, None, None),
        P(("group", "dp", "shard"), None, None, None),
        P("group", None, "shard"),
        P("group", None, "shard"),
    )
    return jax.shard_map(
        body,
        mesh=mesh,
        in_specs=placed,
        out_specs=(
            P(("group", "dp", "shard"), None, None, None),
            P("group", None, "shard"),
            P("group", None, "shard"),
        ),
        check_vma=False,
    )
```

```python
import functools

import jax
import jax.numpy as jnp
from jax import lax
from jax.experimental import pallas as pl
from jax.experimental.pallas import tpu as pltpu
from jax.sharding import PartitionSpec as P

F32 = jnp.float32
BF16 = jnp.bfloat16
VMEM_LIMIT = 16 * 1024 * 1024


def column_shifted(field, cols, by):
    cells = field.shape[0]
    col = lax.broadcasted_iota(jnp.int32, field.shape, 0) % cols
    if by == 0:
        return field
    rolled = pltpu.roll(field, (-by) % cells, 0)
    return jnp.where(col == (cols - 1 if by > 0 else 0), 0.0, rolled)


def fill_taps(dst, field, cols, order):
    cells, chans = field.shape
    zeros = jnp.zeros((cols, dst.shape[1]), dst.dtype)
    dst[0:cols, :] = zeros
    dst[cols + cells : cols + cells + cols, :] = zeros
    for slot, by in enumerate(order):
        dst[cols : cols + cells, slot * chans : (slot + 1) * chans] = column_shifted(
            field, cols, by
        ).astype(dst.dtype)


def join_halves(dst, own, other, half, start, away):
    dst[:, pl.ds(start, half)] = own[...]
    dst[:, pl.ds(away, half)] = other[...]


def place(half):
    mine = lax.axis_index("shard")
    start = pl.multiple_of(mine * half, half)
    away = pl.multiple_of((1 - mine) * half, half)
    return start, away


def first_kernel(
    cols, x_own, x_other, c_own, c_other, w_own, w_other, ready_ref,
    grad_ref, hidden_ref, slope_ref,
    weight, taps, narrow, turned, pre_ref,
):
    cells, chans = x_own.shape
    half = w_own.shape[1]
    start, away = place(half)
    join_halves(weight, w_own, w_other, half, start, away)
    for sample, (x_ref, c_ref) in enumerate(((x_own, c_own), (x_other, c_other))):
        fill_taps(taps, x_ref[...].astype(F32), cols, (-1, 0, 1))
        pre = jnp.zeros((cells, chans), F32)
        for above in range(3):
            pre = pre + jnp.dot(
                taps[above * cols : above * cols + cells, :],
                weight[above * 3 * chans : (above + 1) * 3 * chans, :],
                preferred_element_type=F32,
            )
        pre_ref[...] = pre
        hidden = pre * jax.nn.sigmoid(pre)
        if sample == 0:
            hidden_ref[...] = hidden.astype(BF16)
        turned[:, sample * cells : (sample + 1) * cells] = hidden.T.astype(BF16)
        mine = pre_ref[:, pl.ds(start, half)]
        sg = jax.nn.sigmoid(mine)
        slope_ref[sample * cells : (sample + 1) * cells, :] = sg * (1.0 + mine * (1.0 - sg))
        fill_taps(narrow.at[sample], c_ref[:, pl.ds(start, half)].astype(F32), cols, (1, 0, -1))
    weight_grad(cols, turned, narrow, grad_ref)


def ready_kernel(cols, out_ref):
    out_ref[...] = jnp.zeros(out_ref.shape, F32)


def weight_grad(cols, turned, narrow, grad_ref):
    chans = turned.shape[0]
    half = grad_ref.shape[1]
    cells = turned.shape[1] // 2
    for above in range(3):
        at = (2 - above) * cols
        part = jnp.zeros((chans, 3 * half), F32)
        for sample in range(2):
            part = part + jnp.dot(
                turned[:, sample * cells : (sample + 1) * cells],
                narrow[sample, at : at + cells, :],
                preferred_element_type=F32,
            )
        for left in range(3):
            tap = 3 * above + left
            grad_ref[tap * chans : (tap + 1) * chans, :] = part[
                :, left * half : (left + 1) * half
            ].astype(BF16)


def second_kernel(
    cols, x_own, x_other, c_own, c_other, w_own, w_other, slope_ref,
    grad_ref,
    weight, taps, narrow, turned,
):
    cells, chans = x_own.shape
    half = w_own.shape[1]
    start, away = place(half)
    join_halves(weight, w_own, w_other, half, start, away)
    for sample, (x_ref, c_ref) in enumerate(((x_own, c_own), (x_other, c_other))):
        fill_taps(taps, c_ref[...].astype(F32), cols, (1, 0, -1))
        turned[:, sample * cells : (sample + 1) * cells] = x_ref[...].astype(F32).T.astype(BF16)
        back = jnp.zeros((cells, half), F32)
        for tap in range(9):
            above, left = tap // 3, tap % 3
            at = (2 - above) * cols
            back = back + lax.dot_general(
                taps[at : at + cells, left * chans : (left + 1) * chans],
                weight[pl.ds(pl.multiple_of(tap * chans + start, half), half), :],
                (((1,), (1,)), ((), ())),
                preferred_element_type=F32,
            )
        dpre = back * slope_ref[sample * cells : (sample + 1) * cells, :]
        fill_taps(narrow.at[sample], dpre, cols, (1, 0, -1))
    weight_grad(cols, turned, narrow, grad_ref)


def output_kernel(cols, x_ref, h_ref, w_own, w_other, out_ref, weight, taps):
    cells, chans = x_ref.shape
    half = w_own.shape[1]
    start, away = place(half)
    join_halves(weight, w_own, w_other, half, start, away)
    fill_taps(taps, h_ref[...].astype(F32), cols, (-1, 0, 1))
    total = x_ref[...].astype(F32)
    for above in range(3):
        total = total + jnp.dot(
            taps[above * cols : above * cols + cells, :],
            weight[above * 3 * chans : (above + 1) * 3 * chans, :],
            preferred_element_type=F32,
        )
    out_ref[...] = total.astype(BF16)


def call(kernel, cols, outs, scratch, flops, *args):
    moved = sum(a.size * a.dtype.itemsize for a in args)
    return pl.pallas_call(
        functools.partial(kernel, cols),
        out_shape=outs,
        in_specs=[pl.BlockSpec(memory_space=pltpu.VMEM)] * len(args),
        out_specs=jax.tree.map(lambda _: pl.BlockSpec(memory_space=pltpu.VMEM), outs),
        scratch_shapes=scratch,
        compiler_params=pltpu.CompilerParams(vmem_limit_bytes=VMEM_LIMIT),
        cost_estimate=pl.CostEstimate(flops=flops, bytes_accessed=moved, transcendentals=0),
    )(*args)


def swapped(value, mask):
    pairs = [(d, d ^ mask) for d in range(lax.axis_size("dp"))]
    return lax.ppermute(value, "dp", pairs)


def after(value, *others):
    return lax.optimization_barrier((value, *others))[0]


class Summed:
    def __init__(self, value, scale):
        devices = lax.axis_size("dp")
        bits = devices.bit_length() - 1
        assert devices == 1 << bits
        self.near = min(4, devices)
        self.far = [1 << k for k in range(self.near.bit_length() - 1, bits)]
        if len(self.far) and self.near == 4:
            self.far[0] = 6
        self.rows = value.shape[0] // self.near
        self.value, self.scale = value, scale
        place_dp = lax.axis_index("dp")
        mirrored = place_dp ^ (((place_dp >> 2) & 1) << 1) if self.far and self.near == 4 else place_dp
        self.at = mirrored % self.near

    def quarter(self, index):
        return lax.dynamic_slice_in_dim(self.value, index * self.rows, self.rows, 0)

    def scatter(self):
        sent = [self.quarter(self.at ^ mask) for mask in range(1, self.near)]
        self.came = [swapped(v, mask + 1) for mask, v in enumerate(sent)]

    def add(self):
        total = self.quarter(self.at).astype(F32)
        for came in self.came:
            total = total + came.astype(F32)
        self.sum = total if not self.far else total.astype(BF16)

    def swap(self, *others):
        for k, mask in enumerate(self.far):
            sent = after(self.sum, *others) if k == 0 and others else self.sum
            self.came = [swapped(sent, mask)]
            if k + 1 < len(self.far):
                self.sum = (self.sum.astype(F32) + self.came[0].astype(F32)).astype(BF16)

    def finish(self):
        total = self.sum.astype(F32)
        if self.far:
            total = total + self.came[0].astype(F32)
        self.sum = (total * self.scale).astype(BF16)

    def gather(self, *others):
        sent = after(self.sum, *others) if others else self.sum
        self.came = [swapped(sent, mask) for mask in range(1, self.near)]

    def result(self):
        whole = jnp.zeros(self.value.shape, BF16)
        for mask, piece in enumerate([self.sum] + self.came):
            whole = lax.dynamic_update_slice_in_dim(whole, piece, (self.at ^ mask) * self.rows, 0)
        return whole


def body(inputs, cotangent, conv_first, conv_second):
    _, rows, cols, chans = inputs.shape
    cells = rows * cols
    half = conv_first.shape[2]
    swap = [(0, 1), (1, 0)]
    x_own = inputs.reshape(cells, chans)
    c_own = cotangent.reshape(cells, chans)
    w1_own = conv_first.reshape(9 * chans, half)
    w2_own = conv_second.reshape(9 * chans, half)
    w1_other, x_other, c_other, w2_other = (
        lax.ppermute(v, "shard", swap) for v in (w1_own, x_own, c_own, w2_own)
    )
    unit = 2 * 9 * cells * chans * chans
    weight = pltpu.VMEM((9 * chans, chans), BF16)
    taps = pltpu.VMEM((cells + 2 * cols, 3 * chans), BF16)
    narrow = pltpu.VMEM((2, cells + 2 * cols, 3 * half), BF16)
    turned = pltpu.VMEM((chans, 2 * cells), BF16)
    grad_shape = jax.ShapeDtypeStruct((9 * chans, half), BF16)
    ready = call(ready_kernel, cols, jax.ShapeDtypeStruct((8, 128), F32), [], 4 * unit)
    second, hidden, slope = call(
        first_kernel,
        cols,
        (
            grad_shape,
            jax.ShapeDtypeStruct((cells, chans), BF16),
            jax.ShapeDtypeStruct((2 * cells, half), F32),
        ),
        [weight, taps, narrow, turned, pltpu.VMEM((cells, chans), F32)],
        3 * unit,
        x_own, x_other, c_own, c_other, w1_own, w1_other, ready,
    )
    def make_late():
        return call(
            second_kernel,
            cols,
            grad_shape,
            [weight, taps, narrow, turned],
            2 * unit,
            x_own, x_other, c_own, c_other, w2_own, w2_other, slope,
        )

    outputs = call(
        output_kernel,
        cols,
        jax.ShapeDtypeStruct((cells, chans), BF16),
        [weight, taps],
        unit,
        x_own, hidden, w2_own, w2_other,
    )
    scale = 1.0 / (inputs.shape[0] * lax.axis_size("dp") * lax.axis_size("shard"))
    early, late = Summed(second, scale), None
    early.scatter()
    late = Summed(make_late(), scale)
    late.scatter()
    early.add()
    early.swap()
    late.add()
    late.swap()
    early.finish()
    early.gather()
    late.finish()
    late.gather()
    grad_second, grad_first = early.result(), late.result()
    return (
        outputs.reshape(inputs.shape),
        grad_first.reshape(conv_first.shape),
        grad_second.reshape(conv_second.shape),
    )


def solution(mesh):
    placed = (
        P(("group", "dp", "shard"), None, None, None),
        P(("group", "dp", "shard"), None, None, None),
        P("group", None, "shard"),
        P("group", None, "shard"),
    )
    return jax.shard_map(
        body,
        mesh=mesh,
        in_specs=placed,
        out_specs=(
            P(("group", "dp", "shard"), None, None, None),
            P("group", None, "shard"),
            P("group", None, "shard"),
        ),
        check_vma=False,
    )
```
